128 devices in a mesh: var: 8 (over x, core), smp: 16 (over z, y).
Axes of the slice: x: 4, y: 4, z: 4, core: 2. Of those that a mesh axis runs over, the one named last changes fastest.
Arguments:
- standardized: bfloat16 [8192, 24576], P('smp', 'var'), may hold values from -6 to 6
- weights: float32 [512, 24576], P('smp', 'var'), may hold values from -0.0390625 to 0.0390625
Outputs:
- weights_out: float32 [512, 24576], P('smp', 'var')
- gradient: float32 [512, 24576], P('smp', 'var')
- variance: float32 [24576], P('var')
The draws below stay inside these ranges and needn't reach their ends.
All inputs are finite; a program needn't handle non-finite values.
Results may differ from the reference program's by a relative error of at most 0.034.
Values may be sent and summed in bfloat16 or wider, within the bound.
No kernel may reach another device: no remote copies, remote signals or barrier semaphores. Data moves between devices by JAX's collectives and lax.ppermute only.
A program may use at most 64 MiB of HBM per device.

```python
import math
import jax
import jax.numpy as jnp
from jax import lax

M = 512
ITERS = 2
P_SIZE = 24576
N = 8192


def steps_of(own_key, shape, shards, smallest, largest):
    factor_of, own = 1.0, jax.random.fold_in(own_key, 6)
    for axis_at, blocks in shards:
        heights = jnp.exp(jax.random.uniform(jax.random.fold_in(own, axis_at), (blocks,), jnp.float32, smallest / len(shards), largest / len(shards)))
        factor_of = factor_of * jnp.repeat(heights, shape[axis_at] // blocks).reshape([-1 if axis == axis_at else 1 for axis in range(len(shape))])
    return factor_of


def centred(stream_key, dims, scale, most, shards=(), held_as=jnp.bfloat16):
    values = jax.random.normal(stream_key, dims, jnp.float32) * scale
    if len(shards) > 0:
        values = steps_of(stream_key, dims, shards, -0.22, 0.18) * values
    return jnp.clip(values, min=-most, max=most).astype(held_as)


def setup_inputs(seed: int = 0) -> dict:
    seeds = jax.random.split(jax.random.key(seed), 3)
    return {
        "standardized": centred(seeds[0], (N, P_SIZE), 1.0, 6.0, ((0, 16), (1, 8))),
        "weights": centred(seeds[1], (M, P_SIZE), P_SIZE ** -0.5, 0.0390625, ((0, 16), (1, 8)), jnp.float32),
    }


epsilon = 1e-05
learn_rate = 0.5

def reference(standardized, weights):
    gradient = jnp.zeros_like(weights)
    variance = jnp.zeros((P_SIZE,), jnp.float32)
    for sweep in range(ITERS):
        weights_bf = weights.astype(jnp.bfloat16)
        latent = jnp.dot(standardized, weights_bf.T, preferred_element_type=jnp.float32)
        moment = lax.optimization_barrier(jnp.sum(latent * latent, axis=0))
        normal = (latent * lax.rsqrt(moment / N + epsilon)).astype(jnp.bfloat16)
        coeffs = (jnp.dot(normal.T, standardized, preferred_element_type=jnp.float32) / N).astype(jnp.bfloat16)
        residual = standardized.astype(jnp.float32) - jnp.dot(normal, coeffs, preferred_element_type=jnp.float32)
        variance = lax.optimization_barrier(jnp.sum(residual * residual, axis=0)) / N + epsilon
        scaled = (residual / variance).astype(jnp.bfloat16)
        gradient = jnp.dot(normal.T, scaled, preferred_element_type=jnp.float32) / math.sqrt(N)
        weights = weights + learn_rate / math.sqrt(P_SIZE) * gradient
    return (weights, gradient, variance)
```

```python
import math

import jax
import jax.numpy as jnp
from jax import lax
from jax.sharding import PartitionSpec as P

ITERS = 2


epsilon = 1e-05
learn_rate = 0.5

SIDE = 4
CORES = 2
Y_GROUPS = [[z * SIDE + y for y in range(SIDE)] for z in range(SIDE)]
f32 = jnp.float32
bf16 = jnp.bfloat16


def from_y(piece, step):
    pairs = [(z * SIDE + (y + step) % SIDE, z * SIDE + y) for z in range(SIDE) for y in range(SIDE)]
    return lax.ppermute(piece, "smp", pairs)


def from_z(piece, step):
    pairs = [((z + step) % SIDE * SIDE + y, z * SIDE + y) for z in range(SIDE) for y in range(SIDE)]
    return lax.ppermute(piece, "smp", pairs)


def from_x(piece, step):
    pairs = [((x + step) % SIDE * CORES + c, x * CORES + c) for x in range(SIDE) for c in range(CORES)]
    return lax.ppermute(piece, "var", pairs)


def from_core(piece):
    pairs = [(x * CORES + 1 - c, x * CORES + c) for x in range(SIDE) for c in range(CORES)]
    return lax.ppermute(piece, "var", pairs)


def swap_y(blocks):
    return lax.all_to_all(blocks, "smp", 0, 0, axis_index_groups=Y_GROUPS)


def gather_y(block):
    return swap_y(jnp.broadcast_to(block[None], (SIDE,) + block.shape))


def relative(fetch, block):
    return [block] + [fetch(block, step) for step in (1, 3, 2)]


def in_order(own, one, three, two):
    return [own, one, two, three]


def scatter_sum(fetch, parts):
    sent = [parts[d].astype(bf16) for d in range(SIDE)]
    total = parts[0].astype(f32)
    for step in (1, 3, 2):
        total = total + fetch(sent[SIDE - step], step).astype(f32)
    return total


def sum_all(fetch, block):
    total = block
    for step in (1, 3, 2):
        total = total + fetch(block, step)
    return total


def sum_latent(partial):
    half = partial.shape[0] // CORES
    mine = partial[:half] + from_core(partial[half:].astype(bf16)).astype(f32)
    block = half // SIDE
    own = scatter_sum(from_x, [mine[d * block:(d + 1) * block] for d in range(SIDE)]).astype(bf16)
    mine = jnp.concatenate(in_order(*relative(from_x, own)), axis=0)
    return jnp.concatenate([mine, from_core(mine)], axis=0)


def dot(a, b, dims):
    return lax.dot_general(a, b, (dims, ((), ())), preferred_element_type=f32)


def per_device(standardized, weights):
    smp, var = lax.axis_index("smp"), lax.axis_index("var")
    z, y, x, core = smp // SIDE, smp % SIDE, var // CORES, var % CORES
    rows, cols = standardized.shape
    facs = weights.shape[0]
    all_facs = facs * SIDE * SIDE
    half = cols // 2
    own = half // (SIDE * SIDE)
    wide = own * SIDE
    total_rows = rows * SIDE * SIDE
    total_vars = cols * SIDE * CORES
    rate = learn_rate / math.sqrt(total_vars)

    weights_bf = weights.astype(bf16)
    first = jnp.stack(in_order(*relative(from_z, weights_bf[:, :half])))
    first = jnp.roll(first, z, axis=0)
    second = gather_y(weights_bf[:, half:])
    w_a = gather_y(first).reshape(all_facs, half)
    w_b = jnp.stack(in_order(*relative(from_z, second)), axis=1)
    w_b = jnp.roll(w_b, z, axis=1).reshape(all_facs, half)

    data = standardized.reshape(CORES, SIDE, rows // (CORES * SIDE), cols)
    data = jnp.roll(data, (-core, -x), axis=(0, 1)).reshape(rows, cols)
    x_a, x_b = data[:, :half], data[:, half:]
    x_r = jnp.roll(x_b, -z * wide, axis=1)
    squares = jnp.sum(jnp.square(standardized.astype(f32)), axis=0)

    partial = dot(x_a, w_a, ((1,), (1,))) + dot(x_b, w_b, ((1,), (1,)))
    own_a = lax.dynamic_slice_in_dim(w_a, (y * SIDE + z) * own, own, axis=1)
    own_b = lax.dynamic_slice_in_dim(w_b, (z * SIDE + y) * own, own, axis=1)
    held = jnp.concatenate([own_a, own_b], axis=1).T.astype(f32)

    eye = jnp.eye(all_facs, dtype=f32)
    moved = jnp.zeros((2 * own, all_facs), f32)
    for sweep in range(ITERS):
        latent = sum_latent(partial)

        tall = all_facs // (SIDE * CORES)
        gram = dot(latent, latent, ((0,), (0,)))
        gram = lax.dynamic_slice_in_dim(gram, var * tall, tall, axis=0)
        if sweep == 0:
            extra = squares.reshape(-1, all_facs)
            gram = jnp.concatenate([gram, extra], axis=0)
        gram = sum_all(from_z, sum_all(from_y, gram))
        if sweep == 0:
            squares = gram[tall:].reshape(-1)
            sq_a = lax.dynamic_slice_in_dim(squares, (y * SIDE + z) * own, own)
            sq_b = lax.dynamic_slice_in_dim(squares, half + (z * SIDE + y) * own, own)
            squares = jnp.concatenate([sq_a, sq_b])[:, None]
            gram = gram[:tall]
        gram = jnp.stack(in_order(*relative(from_x, gram)))
        gram = jnp.stack([gram, from_core(gram)])
        gram = jnp.roll(gram, (core, x), axis=(0, 1))
        gram = gram.swapaxes(0, 1).reshape(all_facs, all_facs)

        cross_a = dot(x_a, latent, ((0,), (0,))).astype(bf16).reshape(SIDE, wide, all_facs)
        cross_b = dot(x_r, latent, ((0,), (0,))).reshape(SIDE, wide, all_facs)
        cross_a = jnp.sum(swap_y(cross_a).astype(f32), axis=0)
        cross_b = scatter_sum(from_z, [cross_b[d] for d in range(SIDE)])
        cross_a = jnp.roll(cross_a.reshape(SIDE, own, all_facs), -z, axis=0)
        cross_a = scatter_sum(from_z, [cross_a[d] for d in range(SIDE)])
        cross_b = cross_b.astype(bf16).reshape(SIDE, own, all_facs)
        cross_b = jnp.sum(swap_y(cross_b).astype(f32), axis=0)
        cross = jnp.concatenate([cross_a, cross_b], axis=0)

        diag = gram * eye
        scale = lax.rsqrt(jnp.sum(diag, axis=0, keepdims=True) / total_rows + epsilon)
        scale_t = lax.rsqrt(jnp.sum(diag, axis=1, keepdims=True) / total_rows + epsilon)
        excess = (gram * scale_t * scale - total_rows * eye).astype(bf16)
        coeffs = cross * (scale / total_rows)
        mixed = dot(coeffs.astype(bf16), excess, ((1,), (0,)))
        left = jnp.sum(coeffs * (mixed - total_rows * coeffs), axis=1, keepdims=True)
        variance = jnp.maximum(squares + left, 0.0) / total_rows + epsilon
        gradient = mixed * (-1.0 / math.sqrt(total_rows)) / variance
        moved = moved + gradient

        if sweep + 1 < ITERS:
            held = held + rate * gradient
            new = held.astype(bf16)
            first = jnp.stack(in_order(*relative(from_z, new[:own])))
            first = jnp.roll(first, z, axis=0).reshape(wide, all_facs)
            second = gather_y(new[own:]).reshape(wide, all_facs)
            w_a = gather_y(first).reshape(half, all_facs)
            w_b = jnp.concatenate(in_order(*relative(from_z, second)), axis=0)
            partial = dot(x_a, w_a, ((1,), (0,))) + dot(x_r, w_b, ((1,), (0,)))

    both = jnp.concatenate([moved, gradient], axis=0).astype(bf16).T
    both = both.reshape(SIDE, SIDE, facs, 4 * own).swapaxes(0, 1).reshape(-1, facs, 4 * own)
    line = variance.reshape(1, 2 * own)
    high = line.astype(bf16)
    low = (line - high.astype(f32)).astype(bf16)
    tail = jnp.concatenate([high, low], axis=1)
    tail = jnp.broadcast_to(tail[None], (SIDE * SIDE, 16, 4 * own))
    got = lax.all_to_all(jnp.concatenate([both, tail], axis=1), "smp", 0, 0).astype(f32)

    def spread(part):
        part = part.reshape(SIDE, SIDE, -1, 2, own)
        part_a = part[:, :, :, 0].transpose(2, 1, 0, 3).reshape(-1, half)
        part_b = part[:, :, :, 1].transpose(2, 0, 1, 3).reshape(-1, half)
        return jnp.concatenate([part_a, part_b], axis=1)

    moved = spread(got[:, :facs, :2 * own])
    gradient = spread(got[:, :facs, 2 * own:])
    variance = spread(got[:, facs:facs + 1, :2 * own] + got[:, facs:facs + 1, 2 * own:])
    return (weights + rate * moved, gradient, variance.reshape(-1))


def solution(mesh):
    placed = (P("smp", "var"), P("smp", "var"))
    return jax.shard_map(
        per_device,
        mesh=mesh,
        in_specs=placed,
        out_specs=(P("smp", "var"), P("smp", "var"), P("var")),
        check_vma=False,
    )
```

```python
import math

import jax
import jax.numpy as jnp
from jax import lax
from jax.sharding import PartitionSpec as P

ITERS = 2


epsilon = 1e-05
learn_rate = 0.5

SIDE = 4
CORES = 2
Y_GROUPS = [[z * SIDE + y for y in range(SIDE)] for z in range(SIDE)]
f32 = jnp.float32
bf16 = jnp.bfloat16


def from_y(piece, step):
    pairs = [(z * SIDE + (y + step) % SIDE, z * SIDE + y) for z in range(SIDE) for y in range(SIDE)]
    return lax.ppermute(piece, "smp", pairs)


def from_z(piece, step):
    pairs = [((z + step) % SIDE * SIDE + y, z * SIDE + y) for z in range(SIDE) for y in range(SIDE)]
    return lax.ppermute(piece, "smp", pairs)


def from_x(piece, step):
    pairs = [((x + step) % SIDE * CORES + c, x * CORES + c) for x in range(SIDE) for c in range(CORES)]
    return lax.ppermute(piece, "var", pairs)


def from_core(piece):
    pairs = [(x * CORES + 1 - c, x * CORES + c) for x in range(SIDE) for c in range(CORES)]
    return lax.ppermute(piece, "var", pairs)


def swap_y(blocks):
    return lax.all_to_all(blocks, "smp", 0, 0, axis_index_groups=Y_GROUPS)


def copies(block):
    return jnp.broadcast_to(block[None], (SIDE,) + block.shape)


def relative(fetch, block):
    return [block] + [fetch(block, step) for step in (1, 3, 2)]


def in_order(own, one, three, two):
    return [own, one, two, three]


def total(pieces):
    return sum([piece.astype(f32) for piece in pieces[1:]], pieces[0].astype(f32))


def exchange(fetch, parts):
    return [parts[0]] + [fetch(parts[SIDE - step], step) for step in (1, 3, 2)]


def sum_latent(send, keep, turn, base):
    mine = (keep + from_core(send.astype(bf16)).astype(f32)).astype(bf16)
    mine = dot(total(relative(from_x, mine)).astype(bf16), turn, ((1,), (0,)))
    if base is not None:
        mine = mine + base[:mine.shape[0]].astype(f32)
    mine = mine.astype(bf16)
    return jnp.concatenate([mine, from_core(mine)], axis=0)


def dot(a, b, dims):
    return lax.dot_general(a, b, (dims, ((), ())), preferred_element_type=f32)


def together(*values):
    return lax.optimization_barrier(values)


def pack(plain, exact):
    high = exact.astype(bf16)
    low = (exact - high.astype(f32)).astype(bf16)
    fill = -(plain.shape[0] + 2 * exact.shape[0]) % 16
    return jnp.pad(jnp.concatenate([plain.astype(bf16), high, low], axis=0), ((0, fill), (0, 0)))


def unpack(packed, plain, exact):
    packed = packed.astype(f32)
    return packed[:plain], packed[plain:plain + exact] + packed[plain + exact:plain + 2 * exact]


def per_device(standardized, weights):
    smp, var = lax.axis_index("smp"), lax.axis_index("var")
    z, y, x, core = smp // SIDE, smp % SIDE, var // CORES, var % CORES
    rows, cols = standardized.shape
    facs = weights.shape[0]
    all_facs = facs * SIDE * SIDE
    half = cols // 2
    wide = half // SIDE
    own = wide // SIDE
    tall = all_facs // (SIDE * CORES)
    total_rows = rows * SIDE * SIDE
    total_vars = cols * SIDE * CORES
    rate = learn_rate / math.sqrt(total_vars)

    weights_bf = weights.astype(bf16)
    first = jnp.stack(in_order(*relative(from_z, weights_bf[:, :half])))
    pieces = in_order(*relative(from_y, weights_bf[:, half:]))
    turns = [jnp.stack(pieces[SIDE - turn:] + pieces[:SIDE - turn]) for turn in range(SIDE)]
    second = jnp.where(y < 2, jnp.where(y == 0, turns[0], turns[1]), jnp.where(y == 2, turns[2], turns[3]))
    data, first, second = together(standardized, first, second)

    row = lax.broadcasted_iota(jnp.int32, (all_facs, 1), 0)
    col = lax.broadcasted_iota(jnp.int32, (all_facs, all_facs), 1)
    at = row // (SIDE * facs) * (SIDE * facs) + (row // facs + z) % SIDE * facs + row % facs
    turn = (at == col).astype(bf16)
    at = (row // tall % SIDE + x) % SIDE * CORES + (row // (SIDE * tall) + core) % CORES
    place = (at * tall + row % tall == col).astype(bf16)

    w_b = relative(from_z, second)
    w_a = swap_y(copies(first)).reshape(all_facs, half)

    mid = rows // CORES
    pieces = [lax.dynamic_slice_in_dim(data, (core + c) % CORES * mid, mid, axis=0) for c in range(CORES)]
    data = jnp.concatenate(pieces, axis=0)
    x_a, x_b = data[:, :half], data[:, half:]
    x_r = [lax.dynamic_slice_in_dim(x_b, (z + d) % SIDE * wide, wide, axis=1) for d in range(SIDE)]
    x_r = jnp.concatenate(x_r, axis=1)
    squares = jnp.sum(jnp.square(data.astype(f32)), axis=0).reshape(-1, all_facs)
    w_a, x_a, x_b, x_r, squares, turn, place = together(w_a, x_a, x_b, x_r, squares, turn, place)
    w_b = jnp.stack(in_order(*w_b), axis=1).reshape(all_facs, half)

    partial = dot(x_a, w_a, ((1,), (1,))) + dot(x_b, w_b, ((1,), (1,)))
    send, keep = partial[mid:], partial[:mid]

    latent = None
    for sweep in range(ITERS):
        last = sweep + 1 == ITERS
        latent = sum_latent(send, keep, turn, latent)

        cross_b = dot(x_r, latent, ((0,), (0,))).astype(bf16).reshape(SIDE, wide, all_facs)
        cross_a = dot(x_a, latent, ((0,), (0,))).astype(bf16).reshape(SIDE, wide, all_facs)
        gram = dot(latent, latent, ((0,), (0,)))
        gram = lax.dynamic_slice_in_dim(gram, var * tall, tall, axis=0)
        mine = lax.broadcasted_iota(jnp.int32, (tall, all_facs), 1) - var * tall
        mine = mine == lax.broadcasted_iota(jnp.int32, (tall, all_facs), 0)
        exact = jnp.sum(jnp.where(mine, gram, 0.0), axis=0, keepdims=True)
        if sweep == 0:
            exact = jnp.concatenate([exact, squares], axis=0)
        count = exact.shape[0]
        gram = pack(gram, exact)
        gram = jnp.broadcast_to(gram[None], (SIDE,) + gram.shape)
        cross_a, cross_b = together(jnp.concatenate([cross_a, gram], axis=1), cross_b)
        cross_a = swap_y(cross_a)
        cross_b = total(exchange(from_z, [cross_b[d] for d in range(SIDE)])).astype(bf16)
        cross_a, exact = unpack(jnp.sum(cross_a.astype(f32), axis=0), wide + tall, count)
        cross_a, exact, cross_b = together(cross_a, exact, cross_b)

        if not last:
            cross_a = total(relative(from_z, pack(cross_a, exact)))
            cross_b = jnp.sum(swap_y(copies(cross_b)).astype(f32), axis=0).astype(bf16)
            cross_a, exact = unpack(cross_a, wide + tall, count)
            gram = pack(cross_a[wide:], exact[:1])
            squares = exact[1:].reshape(-1)
            cross_a = cross_a[:wide].astype(bf16)
            gram, cross_a, cross_b = together(gram, cross_a, cross_b)
            cross_a = swap_y(copies(cross_a)).reshape(half, all_facs)
            cross_b = jnp.concatenate(in_order(*relative(from_z, cross_b)), axis=0)
        else:
            parts = [lax.dynamic_slice_in_dim(cross_a, (z + d) % SIDE * own, own) for d in range(SIDE)]
            parts = [pack(jnp.concatenate([part, cross_a[wide:]]), exact) for part in parts]
            cross_a = total(exchange(from_z, parts))
            parts = [lax.dynamic_slice_in_dim(cross_b, (y + d) % SIDE * own, own) for d in range(SIDE)]
            cross_b = total(exchange(from_y, parts))
            cross_a, exact = unpack(cross_a, own + tall, count)
            gram, exact, cross_b = together(cross_a[own:], exact, cross_b)
            gram = pack(gram, exact)
            cross_a = cross_a[:own]
        gram = jnp.stack(in_order(*relative(from_x, gram)))
        gram = jnp.concatenate([gram, from_core(gram)], axis=0)

        diag = jnp.sum(gram[:, tall:].astype(f32), axis=(0, 1))[None]
        gram = gram[:, :tall].reshape(all_facs, all_facs).astype(f32)
        scale = lax.rsqrt(diag / total_rows + epsilon)
        scale_t = jnp.sum(jnp.where(place > 0, scale, 0.0), axis=1, keepdims=True)
        excess = jnp.where(place > 0, diag * scale * scale - total_rows, gram * scale_t * scale)
        excess = (excess * (scale_t / total_rows)).astype(bf16)
        excess = dot(place, excess, ((0,), (0,)))

        def mix(cross):
            return dot(cross.astype(bf16), excess.astype(bf16), ((1,), (0,)))

        def variance_of(cross, mixed, square):
            cross = cross.astype(f32) * scale
            left = jnp.sum(cross * (mixed.astype(f32) - cross), axis=1, keepdims=True) / total_rows
            return jnp.maximum(square[:, None] + left, 0.0) / total_rows + epsilon

        slope = -1.0 / math.sqrt(total_rows)
        start_a, start_b = (y * SIDE + z) * own, (z * SIDE + y) * own
        if not last:
            square_b = jnp.roll(squares[half:], -z * wide)
            mixed_b, cross_b = together(mix(cross_b).astype(bf16), cross_b)
            shrink_b = 1.0 / variance_of(cross_b, mixed_b, square_b)
            w_b = (cross_b.astype(f32) * shrink_b).astype(bf16)
            w_b, shrink_b, cross_a = together(w_b, shrink_b, cross_a)
            mixed_a, cross_a = together(mix(cross_a).astype(bf16), cross_a)
            shrink_a = 1.0 / variance_of(cross_a, mixed_a, squares[:half])
            w_a = (cross_a.astype(f32) * shrink_a).astype(bf16)
            w_a, shrink_a = together(w_a, shrink_a)
            send, keep = [
                dot(x_a[at], w_a, ((1,), (0,))) + dot(x_r[at], w_b, ((1,), (0,)))
                for at in (slice(mid, None), slice(None, mid))
            ]
            turn = (excess * (rate * slope)).astype(bf16)
            moved = []
            for mixed, shrink, start in ((mixed_a, shrink_a, start_a), (mixed_b, shrink_b, y * own)):
                moved.append(
                    lax.dynamic_slice_in_dim(mixed, start, own).astype(f32)
                    * lax.dynamic_slice_in_dim(shrink, start, own)
                    * slope
                )
            moved = jnp.concatenate(moved, axis=0)
        else:
            cross = jnp.concatenate([cross_a, cross_b], axis=0)
            square = [lax.dynamic_slice_in_dim(squares, start, own) for start in (start_a, half + start_b)]
            mixed = mix(cross)
            variance = variance_of(cross, mixed, jnp.concatenate(square))
            gradient = mixed * slope / variance
            moved = moved + gradient

    both = jnp.concatenate([moved, gradient], axis=0).astype(bf16).T
    both = both.reshape(SIDE, SIDE, facs, 4 * own).swapaxes(0, 1).reshape(-1, facs, 4 * own)
    line = variance.reshape(1, 2 * own)
    high = line.astype(bf16)
    low = (line - high.astype(f32)).astype(bf16)
    tail = jnp.concatenate([high, low], axis=1)
    tail = jnp.broadcast_to(tail[None], (SIDE * SIDE, 16, 4 * own))
    got = lax.all_to_all(jnp.concatenate([both, tail], axis=1), "smp", 0, 0).astype(f32)

    def spread(part):
        part = part.reshape(SIDE, SIDE, -1, 2, own)
        part_a = part[:, :, :, 0].transpose(2, 1, 0, 3).reshape(-1, half)
        part_b = part[:, :, :, 1].transpose(2, 0, 1, 3).reshape(-1, half)
        return jnp.concatenate([part_a, part_b], axis=1)

    moved = spread(got[:, :facs, :2 * own])
    gradient = spread(got[:, :facs, 2 * own:])
    variance = spread(got[:, facs:facs + 1, :2 * own] + got[:, facs:facs + 1, 2 * own:])
    return (weights + rate * moved, gradient, variance.reshape(-1))


def solution(mesh):
    placed = (P("smp", "var"), P("smp", "var"))
    return jax.shard_map(
        per_device,
        mesh=mesh,
        in_specs=placed,
        out_specs=(P("smp", "var"), P("smp", "var"), P("var")),
        check_vma=False,
    )
```

```python
import math

import jax
import jax.numpy as jnp
from jax import lax
from jax.experimental import pallas as pl
from jax.experimental.pallas import tpu as pltpu
from jax.sharding import PartitionSpec as P

ITERS = 2


epsilon = 1e-05
learn_rate = 0.5

SIDE = 4
ORDER = (0, 1, 3, 2)
CORES = 2
Y_GROUPS = [[z * SIDE + y for y in range(SIDE)] for z in range(SIDE)]
f32 = jnp.float32
bf16 = jnp.bfloat16


def from_y(piece, step):
    pairs = [(z * SIDE + (y + step) % SIDE, z * SIDE + y) for z in range(SIDE) for y in range(SIDE)]
    return lax.ppermute(piece, "smp", pairs)


def from_z(piece, step):
    pairs = [((z + step) % SIDE * SIDE + y, z * SIDE + y) for z in range(SIDE) for y in range(SIDE)]
    return lax.ppermute(piece, "smp", pairs)


def from_x(piece, step):
    pairs = [((x + step) % SIDE * CORES + c, x * CORES + c) for x in range(SIDE) for c in range(CORES)]
    return lax.ppermute(piece, "var", pairs)


def from_core(piece):
    pairs = [(x * CORES + 1 - c, x * CORES + c) for x in range(SIDE) for c in range(CORES)]
    return lax.ppermute(piece, "var", pairs)


def swap_y(blocks):
    return lax.all_to_all(blocks, "smp", 0, 0, axis_index_groups=Y_GROUPS)


def copies(block):
    return jnp.broadcast_to(block[None], (SIDE,) + block.shape)


def relative(fetch, block):
    return [block] + [fetch(block, step) for step in ORDER[1:]]


def in_order(own, one, three, two):
    return [own, one, two, three]


def total(pieces):
    return sum([piece.astype(f32) for piece in pieces[1:]], pieces[0].astype(f32))


def exchange(fetch, parts):
    return [parts[0]] + [fetch(parts[ORDER.index(SIDE - step)], step) for step in ORDER[1:]]


def sum_latent(send, keep, turn, base):
    mine = (keep + from_core(send.astype(bf16)).astype(f32)).astype(bf16)
    mine = dot(total(relative(from_x, mine)).astype(bf16), turn, ((1,), (0,)))
    if base is not None:
        mine = mine + base[:mine.shape[0]].astype(f32)
    mine = mine.astype(bf16)
    return jnp.concatenate([mine, from_core(mine)], axis=0)


def dot(a, b, dims):
    return lax.dot_general(a, b, (dims, ((), ())), preferred_element_type=f32)


def together(*values):
    return lax.optimization_barrier(values)


def pack(plain, exact):
    high = exact.astype(bf16)
    low = (exact - high.astype(f32)).astype(bf16)
    fill = -(plain.shape[0] + 2 * exact.shape[0]) % 16
    return jnp.pad(jnp.concatenate([plain.astype(bf16), high, low], axis=0), ((0, fill), (0, 0)))


def unpack(packed, plain, exact):
    packed = packed.astype(f32)
    return packed[:plain], packed[plain:plain + exact] + packed[plain + exact:plain + 2 * exact]


def per_device(standardized, weights):
    smp, var = lax.axis_index("smp"), lax.axis_index("var")
    z, y, x, core = smp // SIDE, smp % SIDE, var // CORES, var % CORES
    rows, cols = standardized.shape
    facs = weights.shape[0]
    all_facs = facs * SIDE * SIDE
    half = cols // 2
    wide = half // SIDE
    own = wide // SIDE
    tall = all_facs // (SIDE * CORES)
    total_rows = rows * SIDE * SIDE
    total_vars = cols * SIDE * CORES
    rate = learn_rate / math.sqrt(total_vars)

    weights_bf = weights.astype(bf16)
    first = jnp.stack(in_order(*relative(from_z, weights_bf[:, :half])))
    pieces = in_order(*relative(from_y, weights_bf[:, half:]))
    turns = [jnp.stack(pieces[SIDE - turn:] + pieces[:SIDE - turn]) for turn in range(SIDE)]
    second = jnp.where(y < 2, jnp.where(y == 0, turns[0], turns[1]), jnp.where(y == 2, turns[2], turns[3]))
    data, first, second = together(standardized, copies(first), second)

    row = lax.broadcasted_iota(jnp.int32, (all_facs, 1), 0)
    col = lax.broadcasted_iota(jnp.int32, (all_facs, all_facs), 1)
    at = row // (SIDE * facs) * (SIDE * facs) + (row // facs + z) % SIDE * facs + row % facs
    turn = (at == col).astype(bf16)
    at = (row // tall % SIDE + x) % SIDE * CORES + (row // (SIDE * tall) + core) % CORES
    place = (at * tall + row % tall == col).astype(bf16)

    w_b = relative(from_z, second)
    w_a = swap_y(first).reshape(all_facs, half)

    mid = rows // CORES
    pieces = [lax.dynamic_slice_in_dim(data, (core + c) % CORES * mid, mid, axis=0) for c in range(CORES)]
    data = jnp.concatenate(pieces, axis=0)
    x_a, x_b = data[:, :half], data[:, half:]
    x_r = [lax.dynamic_slice_in_dim(x_b, (z + d) % SIDE * wide, wide, axis=1) for d in ORDER]
    x_r = jnp.concatenate(x_r, axis=1)
    squares = jnp.sum(jnp.square(data.astype(f32)), axis=0).reshape(-1, all_facs)
    w_a, x_a, x_b, x_r, squares, turn, place = together(w_a, x_a, x_b, x_r, squares, turn, place)
    w_b = jnp.stack(in_order(*w_b), axis=1).reshape(all_facs, half)

    partial = dot(x_a, w_a, ((1,), (1,))) + dot(x_b, w_b, ((1,), (1,)))
    send, keep = partial[mid:], partial[:mid]

    latent = None
    for sweep in range(ITERS):
        last = sweep + 1 == ITERS
        if not last:
            squares, send = together(squares, send)
            squares = total(relative(from_y, squares))
        latent = sum_latent(send, keep, turn, latent)
        if not last:
            squares, latent = together(squares, latent)

        gram = dot(latent, latent, ((0,), (0,)))
        gram = lax.dynamic_slice_in_dim(gram, var * tall, tall, axis=0)
        mine = lax.broadcasted_iota(jnp.int32, (tall, all_facs), 1) - var * tall
        mine = mine == lax.broadcasted_iota(jnp.int32, (tall, all_facs), 0)
        exact = jnp.sum(jnp.where(mine, gram, 0.0), axis=0, keepdims=True)
        gram = pack(gram, exact)
        if last:
            gram = pack(*unpack(total(relative(from_y, gram)), tall, 1))

        cross_b = dot(x_r, latent, ((0,), (0,))).astype(bf16).reshape(SIDE, wide, all_facs)
        cross_b = [cross_b[d] for d in range(SIDE)]
        cross_a = dot(x_a, latent, ((0,), (0,))).astype(bf16).reshape(SIDE, wide, all_facs)
        if not last:
            cross_a = jnp.concatenate([cross_a, copies(gram)], axis=1)
            cross_a, *cross_b = together(cross_a, *cross_b)
            cross_a = swap_y(cross_a)
            cross_b = total(exchange(from_z, cross_b)).astype(bf16)
            gram, exact = unpack(jnp.sum(cross_a[:, wide:].astype(f32), axis=0), tall, 1)
            gram = pack(gram, jnp.concatenate([exact, squares], axis=0))
            cross_a = jnp.sum(cross_a[:, :wide].astype(f32), axis=0).astype(bf16)
            gram, cross_a, cross_b = together(gram, cross_a, copies(cross_b))
            gram, exact = unpack(total(relative(from_z, gram)), tall, 1 + squares.shape[0])
            squares = exact[1:].reshape(-1)
            gram = jnp.stack(in_order(*relative(from_x, pack(gram, exact[:1]))))
            cross_a = total(relative(from_z, cross_a)).astype(bf16)
            cross_b = jnp.sum(swap_y(cross_b).astype(f32), axis=0).astype(bf16)
            gram, cross_a, cross_b = together(gram, copies(cross_a), cross_b)
            cross_a = swap_y(cross_a).reshape(half, all_facs)
            cross_b = jnp.concatenate(relative(from_z, cross_b), axis=0)
            squares, cross_a = together(squares, cross_a)
        else:
            gram, cross_a, *cross_b = together(gram, cross_a, *cross_b)
            gram, exact = unpack(total(relative(from_z, gram)), tall, 1)
            gram = jnp.stack(in_order(*relative(from_x, pack(gram, exact))))
            cross_a = jnp.sum(swap_y(cross_a).astype(f32), axis=0).astype(bf16)
            cross_b = total(exchange(from_z, cross_b)).astype(bf16)
            gram, cross_a, cross_b = together(gram, cross_a, cross_b)
            parts = [lax.dynamic_slice_in_dim(cross_a, (z + d) % SIDE * own, own) for d in ORDER]
            cross_a = total(exchange(from_z, parts))
            parts = [lax.dynamic_slice_in_dim(cross_b, (y + d) % SIDE * own, own) for d in ORDER]
            cross_b = total(exchange(from_y, parts))
        gram = jnp.concatenate([gram, from_core(gram)], axis=0)

        diag = jnp.sum(gram[:, tall:].astype(f32), axis=(0, 1))[None]
        gram = gram[:, :tall].reshape(all_facs, all_facs).astype(f32)
        scale = lax.rsqrt(diag / total_rows + epsilon)
        scale_t = jnp.sum(jnp.where(place > 0, scale, 0.0), axis=1, keepdims=True)
        excess = jnp.where(place > 0, diag * scale * scale - total_rows, gram * scale_t * scale)
        excess = (excess * (scale_t / total_rows)).astype(bf16)
        excess = dot(place, excess, ((0,), (0,)))

        def mix(cross):
            return dot(cross.astype(bf16), excess.astype(bf16), ((1,), (0,)))

        def variance_of(cross, mixed, square):
            cross = cross.astype(f32) * scale
            left = jnp.sum(cross * (mixed.astype(f32) - cross), axis=1, keepdims=True) / total_rows
            return jnp.maximum(square[:, None] + left, 0.0) / total_rows + epsilon

        slope = -1.0 / math.sqrt(total_rows)
        start_a, start_b = (y * SIDE + z) * own, (z * SIDE + y) * own
        if not last:
            mixed_a, cross_a = together(mix(cross_a).astype(bf16), cross_a)
            shrink_a = 1.0 / variance_of(cross_a, mixed_a, squares[:half])
            w_a = (cross_a.astype(f32) * shrink_a).astype(bf16)
            w_a, shrink_a, cross_b = together(w_a, shrink_a, cross_b)
            square_b = [lax.dynamic_slice_in_dim(squares, half + (z + d) % SIDE * wide, wide) for d in ORDER]
            mixed_b, cross_b = together(mix(cross_b).astype(bf16), cross_b)
            shrink_b = 1.0 / variance_of(cross_b, mixed_b, jnp.concatenate(square_b))
            w_b = (cross_b.astype(f32) * shrink_b).astype(bf16)
            w_b, shrink_b = together(w_b, shrink_b)
            send, keep = [
                dot(x_a[at], w_a, ((1,), (0,))) + dot(x_r[at], w_b, ((1,), (0,)))
                for at in (slice(mid, None), slice(None, mid))
            ]
            turn = (excess * (rate * slope)).astype(bf16)
            moved = []
            for mixed, shrink, start in ((mixed_a, shrink_a, start_a), (mixed_b, shrink_b, y * own)):
                moved.append(
                    lax.dynamic_slice_in_dim(mixed, start, own).astype(f32)
                    * lax.dynamic_slice_in_dim(shrink, start, own)
                    * slope
                )
            moved = jnp.concatenate(moved, axis=0)
        else:
            cross = jnp.concatenate([cross_a, cross_b], axis=0)
            square = [lax.dynamic_slice_in_dim(squares, start, own) for start in (start_a, half + start_b)]
            mixed = mix(cross)
            variance = variance_of(cross, mixed, jnp.concatenate(square))
            gradient = mixed * slope / variance
            moved = moved + gradient

    both = jnp.concatenate([moved, gradient], axis=0).astype(bf16).T
    both = both.reshape(SIDE, SIDE, facs, 4 * own).swapaxes(0, 1).reshape(-1, facs, 4 * own)
    line = variance.reshape(1, 2 * own)
    high = line.astype(bf16)
    low = (line - high.astype(f32)).astype(bf16)
    tail = jnp.concatenate([high, low], axis=1)
    tail = jnp.broadcast_to(tail[None], (SIDE * SIDE, 16, 4 * own))
    got = lax.all_to_all(jnp.concatenate([both, tail], axis=1), "smp", 0, 0)
    return spread(got, weights, rate)


def spread(got, weights, rate):
    facs, cols = weights.shape
    own = cols // (2 * SIDE * SIDE)

    def kernel(got_ref, weights_ref, moved_ref, gradient_ref, variance_ref):
        for part in range(2):
            for first in range(SIDE):
                span = slice((part * SIDE + first) * SIDE * own, (part * SIDE + first + 1) * SIDE * own)
                ends = [(second, first) if part == 0 else (first, second) for second in range(SIDE)]
                at = [z * SIDE + y for z, y in ends]

                def line(rows, start):
                    pieces = [got_ref[s, rows, start:start + own].astype(f32) for s in at]
                    return jnp.concatenate(pieces, axis=1)

                facs_at, last_at = slice(0, facs), slice(facs, facs + 16)
                moved = line(facs_at, part * own)
                moved_ref[:, span] = weights_ref[:, span] + rate * moved
                gradient_ref[:, span] = line(facs_at, (2 + part) * own)
                both = line(last_at, part * own) + line(last_at, (2 + part) * own)
                variance_ref[:, span] = both[:1]

    moved, gradient, variance = pl.pallas_call(
        kernel,
        out_shape=[
            jax.ShapeDtypeStruct((facs, cols), f32),
            jax.ShapeDtypeStruct((facs, cols), f32),
            jax.ShapeDtypeStruct((1, cols), f32),
        ],
        compiler_params=pltpu.CompilerParams(vmem_limit_bytes=16 * 1024 * 1024),
    )(got, weights)
    return moved, gradient, variance.reshape(-1)


def solution(mesh):
    placed = (P("smp", "var"), P("smp", "var"))
    return jax.shard_map(
        per_device,
        mesh=mesh,
        in_specs=placed,
        out_specs=(P("smp", "var"), P("smp", "var"), P("var")),
        check_vma=False,
    )
```

```python
import math

import jax
import jax.numpy as jnp
from jax import lax
from jax.experimental import pallas as pl
from jax.experimental.pallas import tpu as pltpu
from jax.sharding import PartitionSpec as P

ITERS = 2


epsilon = 1e-05
learn_rate = 0.5

SIDE = 4
ORDER = (0, 1, 3, 2)
CORES = 2
Y_GROUPS = [[z * SIDE + y for y in range(SIDE)] for z in range(SIDE)]
f32 = jnp.float32
bf16 = jnp.bfloat16


def from_y(piece, step):
    pairs = [(z * SIDE + (y + step) % SIDE, z * SIDE + y) for z in range(SIDE) for y in range(SIDE)]
    return lax.ppermute(piece, "smp", pairs)


def from_z(piece, step):
    pairs = [((z + step) % SIDE * SIDE + y, z * SIDE + y) for z in range(SIDE) for y in range(SIDE)]
    return lax.ppermute(piece, "smp", pairs)


def from_x(piece, step):
    pairs = [((x + step) % SIDE * CORES + c, x * CORES + c) for x in range(SIDE) for c in range(CORES)]
    return lax.ppermute(piece, "var", pairs)


def from_core(piece):
    pairs = [(x * CORES + 1 - c, x * CORES + c) for x in range(SIDE) for c in range(CORES)]
    return lax.ppermute(piece, "var", pairs)


def swap_y(blocks):
    return lax.all_to_all(blocks, "smp", 0, 0, axis_index_groups=Y_GROUPS)


def copies(block):
    return jnp.broadcast_to(block[None], (SIDE,) + block.shape)


def relative(fetch, block):
    return [block] + [fetch(block, step) for step in ORDER[1:]]


def in_order(own, one, three, two):
    return [own, one, two, three]


def total(pieces):
    return sum([piece.astype(f32) for piece in pieces[1:]], pieces[0].astype(f32))


def exchange(fetch, parts):
    return [parts[0]] + [fetch(parts[ORDER.index(SIDE - step)], step) for step in ORDER[1:]]


def sum_latent(send, keep, turn, base):
    mine = (keep + from_core(send.astype(bf16)).astype(f32)).astype(bf16)
    mine = dot(total(relative(from_x, mine)).astype(bf16), turn, ((1,), (0,)))
    if base is not None:
        mine = mine + base[:mine.shape[0]].astype(f32)
    mine = mine.astype(bf16)
    return jnp.concatenate([mine, from_core(mine)], axis=0)


def dot(a, b, dims):
    return lax.dot_general(a, b, (dims, ((), ())), preferred_element_type=f32)


def together(*values):
    return lax.optimization_barrier(values)


def pack(plain, exact):
    high = exact.astype(bf16)
    low = (exact - high.astype(f32)).astype(bf16)
    fill = -(plain.shape[0] + 2 * exact.shape[0]) % 16
    return jnp.pad(jnp.concatenate([plain.astype(bf16), high, low], axis=0), ((0, fill), (0, 0)))


def unpack(packed, plain, exact):
    packed = packed.astype(f32)
    return packed[:plain], packed[plain:plain + exact] + packed[plain + exact:plain + 2 * exact]


def per_device(standardized, weights):
    smp, var = lax.axis_index("smp"), lax.axis_index("var")
    z, y, x, core = smp // SIDE, smp % SIDE, var // CORES, var % CORES
    rows, cols = standardized.shape
    facs = weights.shape[0]
    all_facs = facs * SIDE * SIDE
    half = cols // 2
    wide = half // SIDE
    own = wide // SIDE
    tall = all_facs // (SIDE * CORES)
    total_rows = rows * SIDE * SIDE
    total_vars = cols * SIDE * CORES
    rate = learn_rate / math.sqrt(total_vars)

    weights_bf = weights.astype(bf16)
    first = jnp.stack(in_order(*relative(from_z, weights_bf[:, :half])))
    pieces = in_order(*relative(from_y, weights_bf[:, half:]))
    turns = [jnp.stack(pieces[SIDE - turn:] + pieces[:SIDE - turn]) for turn in range(SIDE)]
    second = jnp.where(y < 2, jnp.where(y == 0, turns[0], turns[1]), jnp.where(y == 2, turns[2], turns[3]))
    data, first, second = together(standardized, copies(first), second)

    row = lax.broadcasted_iota(jnp.int32, (all_facs, 1), 0)
    col = lax.broadcasted_iota(jnp.int32, (all_facs, all_facs), 1)
    at = row // (SIDE * facs) * (SIDE * facs) + (row // facs + z) % SIDE * facs + row % facs
    turn = (at == col).astype(bf16)
    at = (row // tall % SIDE + x) % SIDE * CORES + (row // (SIDE * tall) + core) % CORES
    place = (at * tall + row % tall == col).astype(bf16)

    w_b = relative(from_z, second)
    w_a = swap_y(first).reshape(all_facs, half)

    mid = rows // CORES
    pieces = [lax.dynamic_slice_in_dim(data, (core + c) % CORES * mid, mid, axis=0) for c in range(CORES)]
    data = jnp.concatenate(pieces, axis=0)
    x_a, x_b = data[:, :half], data[:, half:]
    x_r = [lax.dynamic_slice_in_dim(x_b, (z + d) % SIDE * wide, wide, axis=1) for d in ORDER]
    x_r = jnp.concatenate(x_r, axis=1)
    squares = jnp.sum(jnp.square(data.astype(f32)), axis=0).reshape(-1, all_facs)
    w_a, x_a, x_b, x_r, squares, turn, place = together(w_a, x_a, x_b, x_r, squares, turn, place)
    w_b = jnp.stack(in_order(*w_b), axis=1).reshape(all_facs, half)

    partial = dot(x_a, w_a, ((1,), (1,))) + dot(x_b, w_b, ((1,), (1,)))
    send, keep = partial[mid:], partial[:mid]

    latent = None
    for sweep in range(ITERS):
        last = sweep + 1 == ITERS
        if not last:
            squares, send = together(squares, send)
            squares = total(relative(from_y, squares))
        latent = sum_latent(send, keep, turn, latent)
        if not last:
            squares, latent = together(squares, latent)

        gram = dot(latent, latent, ((0,), (0,)))
        gram = lax.dynamic_slice_in_dim(gram, var * tall, tall, axis=0)
        mine = lax.broadcasted_iota(jnp.int32, (tall, all_facs), 1) - var * tall
        mine = mine == lax.broadcasted_iota(jnp.int32, (tall, all_facs), 0)
        exact = jnp.sum(jnp.where(mine, gram, 0.0), axis=0, keepdims=True)
        gram = pack(gram, exact)
        if last:
            gram = pack(*unpack(total(relative(from_y, gram)), tall, 1))

        cross_b = dot(x_r, latent, ((0,), (0,))).astype(bf16).reshape(SIDE, wide, all_facs)
        cross_b = [cross_b[d] for d in range(SIDE)]
        cross_a = dot(x_a, latent, ((0,), (0,))).astype(bf16).reshape(SIDE, wide, all_facs)
        if not last:
            cross_a = jnp.concatenate([cross_a, copies(gram)], axis=1)
            cross_a, *cross_b = together(cross_a, *cross_b)
            cross_a = swap_y(cross_a)
            cross_b = total(exchange(from_z, cross_b)).astype(bf16)
            gram, exact = unpack(jnp.sum(cross_a[:, wide:].astype(f32), axis=0), tall, 1)
            gram = pack(gram, jnp.concatenate([exact, squares], axis=0))
            cross_a = jnp.sum(cross_a[:, :wide].astype(f32), axis=0).astype(bf16)
            gram, cross_a, cross_b = together(gram, cross_a, copies(cross_b))
            gram, exact = unpack(total(relative(from_z, gram)), tall, 1 + squares.shape[0])
            squares = exact[1:].reshape(-1)
            gram = jnp.stack(in_order(*relative(from_x, pack(gram, exact[:1]))))
            cross_a = total(relative(from_z, cross_a)).astype(bf16)
            cross_b = swap_y(cross_b)
            gram, cross_a, cross_b = together(gram, copies(cross_a), cross_b)
            cross_b = jnp.sum(cross_b.astype(f32), axis=0).astype(bf16)
            cross_a = swap_y(cross_a).reshape(half, all_facs)
            cross_b = jnp.concatenate(relative(from_z, cross_b), axis=0)
            squares, cross_b = together(squares, cross_b)
        else:
            gram, cross_a, *cross_b = together(gram, cross_a, *cross_b)
            gram, exact = unpack(total(relative(from_z, gram)), tall, 1)
            gram = jnp.stack(in_order(*relative(from_x, pack(gram, exact))))
            cross_a = jnp.sum(swap_y(cross_a).astype(f32), axis=0).astype(bf16)
            cross_b = total(exchange(from_z, cross_b)).astype(bf16)
            gram, cross_a, cross_b = together(gram, cross_a, cross_b)
            parts = [lax.dynamic_slice_in_dim(cross_a, (z + d) % SIDE * own, own) for d in ORDER]
            cross_a = total(exchange(from_z, parts))
            parts = [lax.dynamic_slice_in_dim(cross_b, (y + d) % SIDE * own, own) for d in ORDER]
            cross_b = total(exchange(from_y, parts))
        gram = jnp.concatenate([gram, from_core(gram)], axis=0)

        diag = jnp.sum(gram[:, tall:].astype(f32), axis=(0, 1))[None]
        gram = gram[:, :tall].reshape(all_facs, all_facs).astype(f32)
        scale = lax.rsqrt(diag / total_rows + epsilon)
        scale_t = jnp.sum(jnp.where(place > 0, scale, 0.0), axis=1, keepdims=True)
        excess = jnp.where(place > 0, diag * scale * scale - total_rows, gram * scale_t * scale)
        excess = (excess * (scale_t / total_rows)).astype(bf16)
        excess = dot(place, excess, ((0,), (0,)))

        def mix(cross):
            return dot(cross.astype(bf16), excess.astype(bf16), ((1,), (0,)))

        def variance_of(cross, mixed, square):
            cross = cross.astype(f32) * scale
            left = jnp.sum(cross * (mixed.astype(f32) - cross), axis=1, keepdims=True) / total_rows
            return jnp.maximum(square[:, None] + left, 0.0) / total_rows + epsilon

        slope = -1.0 / math.sqrt(total_rows)
        start_a, start_b = (y * SIDE + z) * own, (z * SIDE + y) * own
        if not last:
            square_b = [lax.dynamic_slice_in_dim(squares, half + (z + d) % SIDE * wide, wide) for d in ORDER]
            mixed_b, cross_b = together(mix(cross_b).astype(bf16), cross_b)
            shrink_b = 1.0 / variance_of(cross_b, mixed_b, jnp.concatenate(square_b))
            w_b = (cross_b.astype(f32) * shrink_b).astype(bf16)
            w_b, shrink_b, cross_a = together(w_b, shrink_b, cross_a)
            mixed_a, cross_a = together(mix(cross_a).astype(bf16), cross_a)
            shrink_a = 1.0 / variance_of(cross_a, mixed_a, squares[:half])
            w_a = (cross_a.astype(f32) * shrink_a).astype(bf16)
            w_a, shrink_a = together(w_a, shrink_a)
            send, keep = [
                dot(x_a[at], w_a, ((1,), (0,))) + dot(x_r[at], w_b, ((1,), (0,)))
                for at in (slice(mid, None), slice(None, mid))
            ]
            turn = (excess * (rate * slope)).astype(bf16)
            moved = []
            for mixed, shrink, start in ((mixed_a, shrink_a, start_a), (mixed_b, shrink_b, y * own)):
                moved.append(
                    lax.dynamic_slice_in_dim(mixed, start, own).astype(f32)
                    * lax.dynamic_slice_in_dim(shrink, start, own)
                    * slope
                )
            moved = jnp.concatenate(moved, axis=0)
        else:
            cross = jnp.concatenate([cross_a, cross_b], axis=0)
            square = [lax.dynamic_slice_in_dim(squares, start, own) for start in (start_a, half + start_b)]
            mixed = mix(cross)
            variance = variance_of(cross, mixed, jnp.concatenate(square))
            gradient = mixed * slope / variance
            moved = moved + gradient

    both = jnp.concatenate([moved, gradient], axis=0).astype(bf16).T
    both = both.reshape(SIDE, SIDE, facs, 4 * own).swapaxes(0, 1).reshape(-1, facs, 4 * own)
    line = variance.reshape(1, 2 * own)
    high = line.astype(bf16)
    low = (line - high.astype(f32)).astype(bf16)
    tail = jnp.concatenate([high, low], axis=1)
    tail = jnp.broadcast_to(tail[None], (SIDE * SIDE, 16, 4 * own))
    got = lax.all_to_all(jnp.concatenate([both, tail], axis=1), "smp", 0, 0)
    return spread(got, weights, rate)


def spread(got, weights, rate):
    facs, cols = weights.shape
    own = cols // (2 * SIDE * SIDE)

    def kernel(got_ref, weights_ref, moved_ref, gradient_ref, variance_ref):
        for part in range(2):
            for first in range(SIDE):
                span = slice((part * SIDE + first) * SIDE * own, (part * SIDE + first + 1) * SIDE * own)
                ends = [(second, first) if part == 0 else (first, second) for second in range(SIDE)]
                at = [z * SIDE + y for z, y in ends]

                def line(rows, start):
                    pieces = [got_ref[s, rows, start:start + own].astype(f32) for s in at]
                    return jnp.concatenate(pieces, axis=1)

                facs_at, last_at = slice(0, facs), slice(facs, facs + 16)
                moved = line(facs_at, part * own)
                moved_ref[:, span] = weights_ref[:, span] + rate * moved
                gradient_ref[:, span] = line(facs_at, (2 + part) * own)
                both = line(last_at, part * own) + line(last_at, (2 + part) * own)
                variance_ref[:, span] = both[:1]

    moved, gradient, variance = pl.pallas_call(
        kernel,
        out_shape=[
            jax.ShapeDtypeStruct((facs, cols), f32),
            jax.ShapeDtypeStruct((facs, cols), f32),
            jax.ShapeDtypeStruct((1, cols), f32),
        ],
        compiler_params=pltpu.CompilerParams(vmem_limit_bytes=16 * 1024 * 1024),
    )(got, weights)
    return moved, gradient, variance.reshape(-1)


def solution(mesh):
    placed = (P("smp", "var"), P("smp", "var"))
    return jax.shard_map(
        per_device,
        mesh=mesh,
        in_specs=placed,
        out_specs=(P("smp", "var"), P("smp", "var"), P("var")),
        check_vma=False,
    )
```

```python
import math

import jax
import jax.numpy as jnp
from jax import lax
from jax.experimental import pallas as pl
from jax.experimental.pallas import tpu as pltpu
from jax.sharding import PartitionSpec as P

ITERS = 2


epsilon = 1e-05
learn_rate = 0.5

SIDE = 4
ORDER = (0, 1, 3, 2)
CORES = 2
Y_GROUPS = [[z * SIDE + y for y in range(SIDE)] for z in range(SIDE)]
f32 = jnp.float32
bf16 = jnp.bfloat16


def from_y(piece, step):
    pairs = [(z * SIDE + (y + step) % SIDE, z * SIDE + y) for z in range(SIDE) for y in range(SIDE)]
    return lax.ppermute(piece, "smp", pairs)


def from_z(piece, step):
    pairs = [((z + step) % SIDE * SIDE + y, z * SIDE + y) for z in range(SIDE) for y in range(SIDE)]
    return lax.ppermute(piece, "smp", pairs)


def from_x(piece, step):
    pairs = [((x + step) % SIDE * CORES + c, x * CORES + c) for x in range(SIDE) for c in range(CORES)]
    return lax.ppermute(piece, "var", pairs)


def from_core(piece):
    pairs = [(x * CORES + 1 - c, x * CORES + c) for x in range(SIDE) for c in range(CORES)]
    return lax.ppermute(piece, "var", pairs)


def swap_y(blocks):
    return lax.all_to_all(blocks, "smp", 0, 0, axis_index_groups=Y_GROUPS)


def copies(block):
    return jnp.broadcast_to(block[None], (SIDE,) + block.shape)


def relative(fetch, block):
    return [block] + [fetch(block, step) for step in ORDER[1:]]


def in_order(own, one, three, two):
    return [own, one, two, three]


def total(pieces):
    return sum([piece.astype(f32) for piece in pieces[1:]], pieces[0].astype(f32))


def exchange(fetch, parts):
    return [parts[0]] + [fetch(parts[ORDER.index(SIDE - step)], step) for step in ORDER[1:]]


def sum_latent(send, keep, turn, base):
    mine = (keep + from_core(send.astype(bf16)).astype(f32)).astype(bf16)
    mine = dot(total(relative(from_x, mine)).astype(bf16), turn, ((1,), (0,)))
    if base is not None:
        mine = mine + base[:mine.shape[0]].astype(f32)
    mine = mine.astype(bf16)
    return jnp.concatenate([mine, from_core(mine)], axis=0)


def dot(a, b, dims):
    return lax.dot_general(a, b, (dims, ((), ())), preferred_element_type=f32)


def together(*values):
    return lax.optimization_barrier(values)


def pack(plain, exact):
    high = exact.astype(bf16)
    low = (exact - high.astype(f32)).astype(bf16)
    fill = -(plain.shape[0] + 2 * exact.shape[0]) % 16
    return jnp.pad(jnp.concatenate([plain.astype(bf16), high, low], axis=0), ((0, fill), (0, 0)))


def unpack(packed, plain, exact):
    packed = packed.astype(f32)
    return packed[:plain], packed[plain:plain + exact] + packed[plain + exact:plain + 2 * exact]


def per_device(standardized, weights):
    smp, var = lax.axis_index("smp"), lax.axis_index("var")
    z, y, x, core = smp // SIDE, smp % SIDE, var // CORES, var % CORES
    rows, cols = standardized.shape
    facs = weights.shape[0]
    all_facs = facs * SIDE * SIDE
    half = cols // 2
    wide = half // SIDE
    own = wide // SIDE
    tall = all_facs // (SIDE * CORES)
    total_rows = rows * SIDE * SIDE
    total_vars = cols * SIDE * CORES
    rate = learn_rate / math.sqrt(total_vars)

    weights_bf = weights.astype(bf16)
    first = jnp.stack(in_order(*relative(from_z, weights_bf[:, :half])))
    pieces = in_order(*relative(from_y, weights_bf[:, half:]))
    turns = [jnp.stack(pieces[SIDE - turn:] + pieces[:SIDE - turn]) for turn in range(SIDE)]
    second = jnp.where(y < 2, jnp.where(y == 0, turns[0], turns[1]), jnp.where(y == 2, turns[2], turns[3]))
    data, first, second = together(standardized, copies(first), second)

    row = lax.broadcasted_iota(jnp.int32, (all_facs, 1), 0)
    col = lax.broadcasted_iota(jnp.int32, (all_facs, all_facs), 1)
    at = row // (SIDE * facs) * (SIDE * facs) + (row // facs + z) % SIDE * facs + row % facs
    turn = (at == col).astype(bf16)
    at = (row // tall % SIDE + x) % SIDE * CORES + (row // (SIDE * tall) + core) % CORES
    place = (at * tall + row % tall == col).astype(bf16)

    w_b = relative(from_z, second)
    w_a = swap_y(first).reshape(all_facs, half)

    mid = rows // CORES
    pieces = [lax.dynamic_slice_in_dim(data, (core + c) % CORES * mid, mid, axis=0) for c in range(CORES)]
    data = jnp.concatenate(pieces, axis=0)
    x_a, x_b = data[:, :half], data[:, half:]
    x_r = [lax.dynamic_slice_in_dim(x_b, (z + d) % SIDE * wide, wide, axis=1) for d in ORDER]
    x_r = jnp.concatenate(x_r, axis=1)
    squares = jnp.sum(jnp.square(data.astype(f32)), axis=0).reshape(-1, all_facs)
    w_a, x_a, x_b, x_r, squares, turn, place = together(w_a, x_a, x_b, x_r, squares, turn, place)
    w_b = jnp.stack(in_order(*w_b), axis=1).reshape(all_facs, half)

    partial = dot(x_a, w_a, ((1,), (1,))) + dot(x_b, w_b, ((1,), (1,)))
    send, keep = partial[mid:], partial[:mid]

    latent = None
    for sweep in range(ITERS):
        last = sweep + 1 == ITERS
        if not last:
            squares, send = together(squares, send)
            squares = total(relative(from_y, squares))
        latent = sum_latent(send, keep, turn, latent)
        if not last:
            squares, latent = together(squares, latent)

        gram = dot(latent, latent, ((0,), (0,)))
        gram = lax.dynamic_slice_in_dim(gram, var * tall, tall, axis=0)
        mine = lax.broadcasted_iota(jnp.int32, (tall, all_facs), 1) - var * tall
        mine = mine == lax.broadcasted_iota(jnp.int32, (tall, all_facs), 0)
        exact = jnp.sum(jnp.where(mine, gram, 0.0), axis=0, keepdims=True)
        gram = pack(gram, exact)
        if last:
            gram = pack(*unpack(total(relative(from_y, gram)), tall, 1))

        cross_b = dot(x_r, latent, ((0,), (0,))).astype(bf16).reshape(SIDE, wide, all_facs)
        cross_b = [cross_b[d] for d in range(SIDE)]
        cross_a = dot(x_a, latent, ((0,), (0,))).astype(bf16).reshape(SIDE, wide, all_facs)
        if not last:
            cross_a = jnp.concatenate([cross_a, copies(gram)], axis=1)
            cross_a, *cross_b = together(cross_a, *cross_b)
            cross_a = swap_y(cross_a)
            cross_b = total(exchange(from_z, cross_b)).astype(bf16)
            gram, exact = unpack(jnp.sum(cross_a[:, wide:].astype(f32), axis=0), tall, 1)
            gram = pack(gram, jnp.concatenate([exact, squares], axis=0))
            cross_a = jnp.sum(cross_a[:, :wide].astype(f32), axis=0).astype(bf16)
            gram, cross_a, cross_b = together(gram, cross_a, copies(cross_b))
            gram, exact = unpack(total(relative(from_z, gram)), tall, 1 + squares.shape[0])
            squares = exact[1:].reshape(-1)
            gram = jnp.stack(in_order(*relative(from_x, pack(gram, exact[:1]))))
            cross_a = total(relative(from_z, cross_a)).astype(bf16)
            cross_b = swap_y(cross_b)
            gram, cross_a, cross_b = together(gram, copies(cross_a), cross_b)
            cross_b = jnp.sum(cross_b.astype(f32), axis=0).astype(bf16)
            cross_a = swap_y(cross_a).reshape(half, all_facs)
            cross_b = jnp.concatenate(relative(from_z, cross_b), axis=0)
            squares, cross_b = together(squares, cross_b)
        else:
            gram, cross_a, *cross_b = together(gram, cross_a, *cross_b)
            gram, exact = unpack(total(relative(from_z, gram)), tall, 1)
            gram = jnp.stack(in_order(*relative(from_x, pack(gram, exact))))
            cross_a = jnp.sum(swap_y(cross_a).astype(f32), axis=0).astype(bf16)
            cross_b = total(exchange(from_z, cross_b)).astype(bf16)
            gram, cross_a = together(gram, cross_a)
            parts = [lax.dynamic_slice_in_dim(cross_a, (z + d) % SIDE * own, own) for d in ORDER]
            cross_a = total(exchange(from_z, parts))
            parts = [lax.dynamic_slice_in_dim(cross_b, (y + d) % SIDE * own, own) for d in ORDER]
            cross_b = total(exchange(from_y, parts))
        gram = jnp.concatenate([gram, from_core(gram)], axis=0)

        diag = jnp.sum(gram[:, tall:].astype(f32), axis=(0, 1))[None]
        gram = gram[:, :tall].reshape(all_facs, all_facs).astype(f32)
        scale = lax.rsqrt(diag / total_rows + epsilon)
        scale_t = jnp.sum(jnp.where(place > 0, scale, 0.0), axis=1, keepdims=True)
        excess = jnp.where(place > 0, diag * scale * scale - total_rows, gram * scale_t * scale)
        excess = (excess * (scale_t / total_rows)).astype(bf16)
        excess = dot(place, excess, ((0,), (0,)))

        def mix(cross):
            return dot(cross.astype(bf16), excess.astype(bf16), ((1,), (0,)))

        def variance_of(cross, mixed, square):
            cross = cross.astype(f32) * scale
            left = jnp.sum(cross * (mixed.astype(f32) - cross), axis=1, keepdims=True) / total_rows
            return jnp.maximum(square[:, None] + left, 0.0) / total_rows + epsilon

        slope = -1.0 / math.sqrt(total_rows)
        start_a, start_b = (y * SIDE + z) * own, (z * SIDE + y) * own
        if not last:
            square_b = [lax.dynamic_slice_in_dim(squares, half + (z + d) % SIDE * wide, wide) for d in ORDER]
            mixed_b, cross_b = together(mix(cross_b).astype(bf16), cross_b)
            shrink_b = 1.0 / variance_of(cross_b, mixed_b, jnp.concatenate(square_b))
            w_b = (cross_b.astype(f32) * shrink_b).astype(bf16)
            w_b, shrink_b, cross_a = together(w_b, shrink_b, cross_a)
            mixed_a, cross_a = together(mix(cross_a).astype(bf16), cross_a)
            shrink_a = 1.0 / variance_of(cross_a, mixed_a, squares[:half])
            w_a = (cross_a.astype(f32) * shrink_a).astype(bf16)
            w_a, shrink_a = together(w_a, shrink_a)
            send, keep = [
                dot(x_a[at], w_a, ((1,), (0,))) + dot(x_r[at], w_b, ((1,), (0,)))
                for at in (slice(mid, None), slice(None, mid))
            ]
            turn = (excess * (rate * slope)).astype(bf16)
            moved = []
            for mixed, shrink, start in ((mixed_a, shrink_a, start_a), (mixed_b, shrink_b, y * own)):
                moved.append(
                    lax.dynamic_slice_in_dim(mixed, start, own).astype(f32)
                    * lax.dynamic_slice_in_dim(shrink, start, own)
                    * slope
                )
            moved = jnp.concatenate(moved, axis=0)
        else:
            cross = jnp.concatenate([cross_a, cross_b], axis=0)
            square = [lax.dynamic_slice_in_dim(squares, start, own) for start in (start_a, half + start_b)]
            mixed = mix(cross)
            variance = variance_of(cross, mixed, jnp.concatenate(square))
            gradient = mixed * slope / variance
            moved = moved + gradient

    both = jnp.concatenate([moved, gradient], axis=0).astype(bf16).T
    both = both.reshape(SIDE, SIDE, facs, 4 * own).swapaxes(0, 1).reshape(-1, facs, 4 * own)
    line = variance.reshape(1, 2 * own)
    high = line.astype(bf16)
    low = (line - high.astype(f32)).astype(bf16)
    tail = jnp.concatenate([high, low], axis=1)
    tail = jnp.broadcast_to(tail[None], (SIDE * SIDE, 16, 4 * own))
    got = lax.all_to_all(jnp.concatenate([both, tail], axis=1), "smp", 0, 0)
    return spread(got, weights, rate)


def spread(got, weights, rate):
    facs, cols = weights.shape
    own = cols // (2 * SIDE * SIDE)

    def kernel(got_ref, weights_ref, moved_ref, gradient_ref, variance_ref):
        for part in range(2):
            for first in range(SIDE):
                span = slice((part * SIDE + first) * SIDE * own, (part * SIDE + first + 1) * SIDE * own)
                ends = [(second, first) if part == 0 else (first, second) for second in range(SIDE)]
                at = [z * SIDE + y for z, y in ends]

                def line(rows, start):
                    pieces = [got_ref[s, rows, start:start + own].astype(f32) for s in at]
                    return jnp.concatenate(pieces, axis=1)

                facs_at, last_at = slice(0, facs), slice(facs, facs + 16)
                moved = line(facs_at, part * own)
                moved_ref[:, span] = weights_ref[:, span] + rate * moved
                gradient_ref[:, span] = line(facs_at, (2 + part) * own)
                both = line(last_at, part * own) + line(last_at, (2 + part) * own)
                variance_ref[:, span] = both[:1]

    moved, gradient, variance = pl.pallas_call(
        kernel,
        out_shape=[
            jax.ShapeDtypeStruct((facs, cols), f32),
            jax.ShapeDtypeStruct((facs, cols), f32),
            jax.ShapeDtypeStruct((1, cols), f32),
        ],
        compiler_params=pltpu.CompilerParams(vmem_limit_bytes=16 * 1024 * 1024),
    )(got, weights)
    return moved, gradient, variance.reshape(-1)


def solution(mesh):
    placed = (P("smp", "var"), P("smp", "var"))
    return jax.shard_map(
        per_device,
        mesh=mesh,
        in_specs=placed,
        out_specs=(P("smp", "var"), P("smp", "var"), P("var")),
        check_vma=False,
    )
```
